32 devices in a mesh: dp: 16 (over z, x, core), tensor: 2 (over y).
Axes of the slice: x: 2, y: 2, z: 4, core: 2. Of those that a mesh axis runs over, the one named last changes fastest.
Arguments:
- hidden_in: bfloat16 [4096, 1536], P(('dp', 'tensor')), may hold values from -6 to 6
- out_grad: bfloat16 [4096, 1536], P(('dp', 'tensor')), may hold values from -6 to 6
- routes_first: int32 [4096, 6], P('dp'), may hold values from 0 to 15, all different within a row; in each aligned block of 256 rows (0 to 255, 256 to 511, ...) at most 128 rows name the same one
- routes_second: int32 [4096, 6], P('dp'), may hold values from 0 to 15, all different within a row; in each aligned block of 256 rows (0 to 255, 256 to 511, ...) at most 128 rows name the same one
- in_gate: bfloat16 [1536, 3072], P('dp', 'tensor'), may hold values from -0.15625 to 0.15625
- in_value: bfloat16 [1536, 3072], P('dp', 'tensor'), may hold values from -0.15625 to 0.15625
- in_state: bfloat16 [1536, 256], P('dp', 'tensor'), may hold values from -0.15625 to 0.15625
- in_step: bfloat16 [1536, 48], P('dp', 'tensor'), may hold values from -0.15625 to 0.15625
- mix_output: bfloat16 [3072, 1536], P('tensor', 'dp'), may hold values from -0.109375 to 0.109375
- attn_query: bfloat16 [1536, 1536], P('dp', 'tensor'), may hold values from -0.15625 to 0.15625
- attention_key_matrix: bfloat16 [1536, 512], P('dp', 'tensor'), may hold values from -0.15625 to 0.15625
- attention_value_matrix: bfloat16 [1536, 512], P('dp', 'tensor'), may hold values from -0.15625 to 0.15625
- attn_output: bfloat16 [1536, 1536], P('tensor', 'dp'), may hold values from -1.25 to 1.25
- shared_gate_one: bfloat16 [1536, 1024], P('dp', 'tensor'), may hold values from -0.15625 to 0.15625
- shared_up_one: bfloat16 [1536, 1024], P('dp', 'tensor'), may hold values from -0.15625 to 0.15625
- shared_down_one: bfloat16 [1024, 1536], P('tensor', 'dp'), may hold values from -0.375 to 0.375
- shared_gate_two: bfloat16 [1536, 1024], P('dp', 'tensor'), may hold values from -0.15625 to 0.15625
- shared_up_two: bfloat16 [1536, 1024], P('dp', 'tensor'), may hold values from -0.15625 to 0.15625
- shared_down_two: bfloat16 [1024, 1536], P('tensor', 'dp'), may hold values from -0.375 to 0.375
- expert_gate_one: bfloat16 [16, 1536, 512], P('dp', None, 'tensor'), may hold values from -0.15625 to 0.15625
- expert_up_one: bfloat16 [16, 1536, 512], P('dp', None, 'tensor'), may hold values from -0.15625 to 0.15625
- expert_down_one: bfloat16 [16, 512, 1536], P('dp', 'tensor'), may hold values from -0.5 to 0.5
- expert_gate_two: bfloat16 [16, 1536, 512], P('dp', None, 'tensor'), may hold values from -0.15625 to 0.15625
- expert_up_two: bfloat16 [16, 1536, 512], P('dp', None, 'tensor'), may hold values from -0.15625 to 0.15625
- expert_down_two: bfloat16 [16, 512, 1536], P('dp', 'tensor'), may hold values from -0.5 to 0.5
- router_one: bfloat16 [1536, 16], replicated, may hold values from -0.078125 to 0.078125
- router_two: bfloat16 [1536, 16], replicated, may hold values from -0.078125 to 0.078125
- norm_mix: float32 [1536], replicated, may hold values from 0.5 to 1.5
- norm_moe_one: float32 [1536], replicated, may hold values from 0.5 to 1.5
- norm_attn: float32 [1536], replicated, may hold values from 0.5 to 1.5
- norm_moe_two: float32 [1536], replicated, may hold values from 0.5 to 1.5
- gated_norm: float32 [3072], replicated, may hold values from 0.5 to 1.5
- conv_value_weight: float32 [4, 3072], replicated, may hold values from -3 to 3
- conv_value_bias: float32 [3072], replicated, may hold values from -0.5 to 0.5
- conv_state_weight: float32 [4, 256], replicated, may hold values from -3 to 3
- conv_state_bias: float32 [256], replicated, may hold values from -0.5 to 0.5
- step_bias: float32 [48], replicated, may hold values from -6 to -2
- decay_log: float32 [48], replicated, may hold values from 0 to 1.5
- skip_gain: float32 [48], replicated, may hold values from 0.5 to 1.5
Outputs:
- block_out: float32 [4096, 1536], P(('dp', 'tensor'))
- input_grad: float32 [4096, 1536], P(('dp', 'tensor'))
- grad_in_gate: float32 [1536, 3072], P('dp', 'tensor')
- grad_in_value: float32 [1536, 3072], P('dp', 'tensor')
- grad_in_state: float32 [1536, 256], P('dp', 'tensor')
- grad_in_step: float32 [1536, 48], P('dp', 'tensor')
- grad_mix_output: float32 [3072, 1536], P('tensor', 'dp')
- grad_attn_query: float32 [1536, 1536], P('dp', 'tensor')
- grad_attn_key: float32 [1536, 512], P('dp', 'tensor')
- grad_attn_value: float32 [1536, 512], P('dp', 'tensor')
- grad_attn_output: float32 [1536, 1536], P('tensor', 'dp')
- grad_shared_gate_one: float32 [1536, 1024], P('dp', 'tensor')
- grad_shared_up_one: float32 [1536, 1024], P('dp', 'tensor')
- grad_shared_down_one: float32 [1024, 1536], P('tensor', 'dp')
- grad_shared_gate_two: float32 [1536, 1024], P('dp', 'tensor')
- grad_shared_up_two: float32 [1536, 1024], P('dp', 'tensor')
- grad_shared_down_two: float32 [1024, 1536], P('tensor', 'dp')
- grad_expert_gate_one: float32 [16, 1536, 512], P('dp', None, 'tensor')
- grad_expert_up_one: float32 [16, 1536, 512], P('dp', None, 'tensor')
- grad_expert_down_one: float32 [16, 512, 1536], P('dp', 'tensor')
- grad_expert_gate_two: float32 [16, 1536, 512], P('dp', None, 'tensor')
- grad_expert_up_two: float32 [16, 1536, 512], P('dp', None, 'tensor')
- grad_expert_down_two: float32 [16, 512, 1536], P('dp', 'tensor')
- grad_router_one: float32 [1536, 16], replicated
- grad_router_two: float32 [1536, 16], replicated
- grad_norm_mix: float32 [1536], replicated
- grad_norm_moe_one: float32 [1536], replicated
- grad_norm_attn: float32 [1536], replicated
- grad_norm_moe_two: float32 [1536], replicated
- grad_gated_norm: float32 [3072], replicated
- grad_conv_value_weight: float32 [4, 3072], replicated
- grad_conv_value_bias: float32 [3072], replicated
- grad_conv_state_weight: float32 [4, 256], replicated
- grad_conv_state_bias: float32 [256], replicated
- grad_step_bias: float32 [48], replicated
- grad_decay_log: float32 [48], replicated
- grad_skip_gain: float32 [48], replicated
The draws below stay inside these ranges and needn't reach their ends.
Inputs may be any that keep to these rules, and one draw needn't show every extreme that they name: `routes_first`: each row names 6 different experts. In the 256 rows of one sequence no expert is named more than 128 times, and in some sequence one expert is named exactly 128 times. `routes_second`: as for routes_first.
All inputs are finite; a program needn't handle non-finite values.
Results may differ from the reference program's by a relative error of at most 0.039.
Values may be sent and summed in bfloat16 or wider, within the bound.
No kernel may reach another device: no remote copies, remote signals or barrier semaphores. Data moves between devices by JAX's collectives and lax.ppermute only.
A program may use at most 384 MiB of HBM per device.

```python
import math
import jax
import jax.numpy as jnp
import numpy as np
from jax import lax

MODEL_WIDTH = 1536
MH = 48
NS = 128
KC = 4
CH = 128
QUERY_HEADS = 12
KEY_VALUE_HEADS = 4
HEAD_SIZE = 128
FF = 512
FS = 1024
TOP = 6
LEN = 256
DI = 3072
EXPERTS = 16
CAP = 128
TOKENS = 4096
N_DP = 16


def shard_levels(rng, dims, cuts, low, high):
    level, own = 1.0, jax.random.fold_in(rng, 6)
    for axis_at, parts in cuts:
        steps = jnp.exp(jax.random.uniform(jax.random.fold_in(own, axis_at), (parts,), jnp.float32, low / len(cuts), high / len(cuts)))
        level = level * jnp.repeat(steps, dims[axis_at] // parts).reshape([-1 if axis == axis_at else 1 for axis in range(len(dims))])
    return level


def shared_out(rng, own, number, rows, amount, top, bound, skew):
    order = jax.random.permutation(rng, amount)
    heavy_load, common = shares(amount, rows * top, bound, skew, True), shares(amount, rows * top, bound, skew, False)
    places = jnp.arange(amount)

    def named(sizes, rotation):
        used = int((sizes > 0).sum())
        fixed = max(1, used // 4)
        moved = fixed + (places - fixed + rotation * (used - fixed)) % max(1, amount - fixed)
        return jnp.zeros((amount,), jnp.int32).at[order[jnp.where(places < fixed, places, moved)]].set(jnp.asarray(sizes, jnp.int32))

    sizes = jnp.where(number % 4 == 0, named(heavy_load, number // 4), named(common, number - number // 4 - 1))
    mixed = jax.random.permutation(jax.random.fold_in(own, 3), amount)
    donor, receiver = mixed[0:amount // 2 * 2:2], mixed[1:amount // 2 * 2:2]
    room = jnp.minimum(sizes[donor] - 1, bound - sizes[receiver]) // 2
    room = jnp.where((donor == order[0]) | (receiver == order[0]) | (sizes[receiver] == 0), 0, jnp.maximum(room, 0))
    moved = jax.random.randint(jax.random.fold_in(own, 4), (amount // 2,), 0, 1 << 20) % (room + 1)
    sizes = sizes.at[donor].add(-moved).at[receiver].add(moved)
    members = jnp.searchsorted(jnp.cumsum(sizes), jnp.arange(rows * top), side="right").astype(jnp.int32)
    grid = members.reshape(top, rows).T
    grid = grid[jax.random.permutation(jax.random.fold_in(own, 1), rows)]
    rotation = jax.random.randint(jax.random.fold_in(own, 2), (rows, 1), 0, top)
    return jnp.take_along_axis(grid, (jnp.arange(top)[None, :] + rotation) % top, axis=1)


def shares(count, total, limit, skew, full):
    weights = [(1 << 20) // math.isqrt(rank ** skew) + 1 for rank in range(1, count + 1)]
    largest = limit if full else min(limit, max(-(-total // count), total * weights[0] // sum(weights)))
    least = 1 if total - largest >= count - 1 else 0
    holding, rest = [largest] + [least] * (count - 1), total - largest - least * (count - 1)
    while rest > 0:
        free = [i for i in range(1, count) if holding[i] < largest] or [i for i in range(1, count) if holding[i] < limit]
        whole, remaining = sum([weights[i] for i in free]), rest
        for i in free:
            extra = min(limit - holding[i], max(1, remaining * weights[i] // whole), rest)
            holding[i] = holding[i] + extra
            rest = rest - extra
    return np.array(holding)


def gaussian(key, extent, scale, limit, pieces=(), held_as=jnp.bfloat16):
    loudness = shard_levels(key, extent, pieces, -0.22, 0.18) if pieces else 1.0
    result = jax.random.normal(key, extent, jnp.float32) * scale * loudness
    return jnp.minimum(jnp.maximum(result, -limit), limit).astype(held_as)


def setup_inputs(seed: int = 0) -> dict:
    splits = jax.random.split(jax.random.key(seed), 40)
    hidden_in = gaussian(splits[0], (TOKENS, MODEL_WIDTH), 1.0, 6.0, ((0, 32),))
    out_grad = gaussian(splits[1], (TOKENS, MODEL_WIDTH), 1.0, 6.0, ((0, 32),))
    routes_first_keys = jax.random.split(jax.random.fold_in(splits[2], 1), TOKENS // LEN)
    routes_first_turns = jax.random.permutation(jax.random.fold_in(splits[2], 3), TOKENS // LEN)
    routes_first = jax.vmap(lambda own, number: shared_out(jax.random.fold_in(splits[2], 2), own, number, LEN, EXPERTS, TOP, CAP, 1))(routes_first_keys, routes_first_turns).reshape((TOKENS, TOP))
    routes_second_keys = jax.random.split(jax.random.fold_in(splits[3], 1), TOKENS // LEN)
    routes_second_turns = jax.random.permutation(jax.random.fold_in(splits[3], 3), TOKENS // LEN)
    routes_second = jax.vmap(lambda own, number: shared_out(jax.random.fold_in(splits[3], 2), own, number, LEN, EXPERTS, TOP, CAP, 1))(routes_second_keys, routes_second_turns).reshape((TOKENS, TOP))
    in_gate = gaussian(splits[4], (MODEL_WIDTH, DI), MODEL_WIDTH ** -0.5, 0.15625, ((0, 16), (1, 2)))
    in_value = gaussian(splits[5], (MODEL_WIDTH, DI), MODEL_WIDTH ** -0.5, 0.15625, ((0, 16), (1, 2)))
    in_state = gaussian(splits[6], (MODEL_WIDTH, 2 * NS), MODEL_WIDTH ** -0.5, 0.15625, ((0, 16), (1, 2)))
    in_step = gaussian(splits[7], (MODEL_WIDTH, MH), MODEL_WIDTH ** -0.5, 0.15625, ((0, 16), (1, 2)))
    mix_output = gaussian(splits[8], (DI, MODEL_WIDTH), DI ** -0.5, 0.109375, ((0, 2), (1, 16)))
    attn_query = gaussian(splits[9], (MODEL_WIDTH, QUERY_HEADS * HEAD_SIZE), MODEL_WIDTH ** -0.5, 0.15625, ((0, 16), (1, 2)))
    attention_key_matrix = gaussian(splits[10], (MODEL_WIDTH, KEY_VALUE_HEADS * HEAD_SIZE), MODEL_WIDTH ** -0.5, 0.15625, ((0, 16), (1, 2)))
    attention_value_matrix = gaussian(splits[11], (MODEL_WIDTH, KEY_VALUE_HEADS * HEAD_SIZE), MODEL_WIDTH ** -0.5, 0.15625, ((0, 16), (1, 2)))
    attn_output = gaussian(splits[12], (QUERY_HEADS * HEAD_SIZE, MODEL_WIDTH), (max(QUERY_HEADS * HEAD_SIZE // 64, 4)) ** -0.5, 1.25, ((0, 2), (1, 16)))
    shared_gate_one = gaussian(splits[13], (MODEL_WIDTH, FS), MODEL_WIDTH ** -0.5, 0.15625, ((0, 16), (1, 2)))
    shared_up_one = gaussian(splits[14], (MODEL_WIDTH, FS), MODEL_WIDTH ** -0.5, 0.15625, ((0, 16), (1, 2)))
    shared_down_one = gaussian(splits[15], (FS, MODEL_WIDTH), (FS // 4) ** -0.5, 0.375, ((0, 2), (1, 16)))
    shared_gate_two = gaussian(splits[16], (MODEL_WIDTH, FS), MODEL_WIDTH ** -0.5, 0.15625, ((0, 16), (1, 2)))
    shared_up_two = gaussian(splits[17], (MODEL_WIDTH, FS), MODEL_WIDTH ** -0.5, 0.15625, ((0, 16), (1, 2)))
    shared_down_two = gaussian(splits[18], (FS, MODEL_WIDTH), (FS // 4) ** -0.5, 0.375, ((0, 2), (1, 16)))
    expert_gate_one = gaussian(splits[19], (EXPERTS, MODEL_WIDTH, FF), MODEL_WIDTH ** -0.5, 0.15625, ((0, 16), (2, 2)))
    expert_up_one = gaussian(splits[20], (EXPERTS, MODEL_WIDTH, FF), MODEL_WIDTH ** -0.5, 0.15625, ((0, 16), (2, 2)))
    expert_down_one = gaussian(splits[21], (EXPERTS, FF, MODEL_WIDTH), (FF // 4) ** -0.5, 0.5, ((0, 16), (1, 2)))
    expert_gate_two = gaussian(splits[22], (EXPERTS, MODEL_WIDTH, FF), MODEL_WIDTH ** -0.5, 0.15625, ((0, 16), (2, 2)))
    expert_up_two = gaussian(splits[23], (EXPERTS, MODEL_WIDTH, FF), MODEL_WIDTH ** -0.5, 0.15625, ((0, 16), (2, 2)))
    expert_down_two = gaussian(splits[24], (EXPERTS, FF, MODEL_WIDTH), (FF // 4) ** -0.5, 0.5, ((0, 16), (1, 2)))
    router_one = gaussian(splits[25], (MODEL_WIDTH, EXPERTS), (4 * MODEL_WIDTH) ** -0.5, 0.078125)
    router_two = gaussian(splits[26], (MODEL_WIDTH, EXPERTS), (4 * MODEL_WIDTH) ** -0.5, 0.078125)
    norm_mix = jnp.clip(1.0 + 0.1 * jax.random.normal(splits[27], (MODEL_WIDTH,), jnp.float32), 0.5, 1.5)
    norm_moe_one = jnp.clip(1.0 + 0.1 * jax.random.normal(splits[28], (MODEL_WIDTH,), jnp.float32), 0.5, 1.5)
    norm_attn = jnp.clip(1.0 + 0.1 * jax.random.normal(splits[29], (MODEL_WIDTH,), jnp.float32), 0.5, 1.5)
    norm_moe_two = jnp.clip(1.0 + 0.1 * jax.random.normal(splits[30], (MODEL_WIDTH,), jnp.float32), 0.5, 1.5)
    gated_norm = jnp.clip(1.0 + 0.1 * jax.random.normal(splits[31], (DI,), jnp.float32), 0.5, 1.5)
    conv_value_weight = gaussian(splits[32], (KC, DI), 0.5, 3.0, (), jnp.float32)
    conv_value_bias = jnp.clip(jax.random.uniform(splits[33], (DI,), jnp.float32, -0.5, 0.5), -0.5, 0.5)
    conv_state_weight = gaussian(splits[34], (KC, 2 * NS), 0.5, 3.0, (), jnp.float32)
    conv_state_bias = jnp.clip(jax.random.uniform(splits[35], (2 * NS,), jnp.float32, -0.5, 0.5), -0.5, 0.5)
    step_bias = jnp.clip(jax.random.uniform(splits[36], (MH,), jnp.float32, -6.0, -2.0), -6.0, -2.0)
    decay_log = jnp.clip(jax.random.uniform(splits[37], (MH,), jnp.float32, 0.0, 1.5), 0.0, 1.5)
    skip_gain = jnp.clip(jax.random.uniform(splits[38], (MH,), jnp.float32, 0.5, 1.5), 0.5, 1.5)
    return dict(hidden_in=hidden_in, out_grad=out_grad, routes_first=routes_first, routes_second=routes_second, in_gate=in_gate, in_value=in_value, in_state=in_state, in_step=in_step, mix_output=mix_output, attn_query=attn_query, attention_key_matrix=attention_key_matrix, attention_value_matrix=attention_value_matrix, attn_output=attn_output, shared_gate_one=shared_gate_one, shared_up_one=shared_up_one, shared_down_one=shared_down_one, shared_gate_two=shared_gate_two, shared_up_two=shared_up_two, shared_down_two=shared_down_two, expert_gate_one=expert_gate_one, expert_up_one=expert_up_one, expert_down_one=expert_down_one, expert_gate_two=expert_gate_two, expert_up_two=expert_up_two, expert_down_two=expert_down_two, router_one=router_one, router_two=router_two, norm_mix=norm_mix, norm_moe_one=norm_moe_one, norm_attn=norm_attn, norm_moe_two=norm_moe_two, gated_norm=gated_norm, conv_value_weight=conv_value_weight, conv_value_bias=conv_value_bias, conv_state_weight=conv_state_weight, conv_state_bias=conv_state_bias, step_bias=step_bias, decay_log=decay_log, skip_gain=skip_gain)


EPS = 1e-05
HIGH = lax.Precision.HIGHEST

@jax.custom_vjp
def reduced_input(v):
    return lax.optimization_barrier(v.astype(jnp.bfloat16)).astype(jnp.float32)

@jax.custom_vjp
def reduced_gradient(v):
    return v

def low_keep(v):
    return (reduced_input(v), None)

def low_pass(kept, grad):
    return (grad,)

def back_keep(v):
    return (v, None)

def back_low(kept, grad):
    return (reduced_input(grad),)
reduced_input.defvjp(low_keep, low_pass)
reduced_gradient.defvjp(back_keep, back_low)

def score_product(left, right):
    return jnp.dot(left, right, precision=HIGH, preferred_element_type=jnp.float32)

def rms_norm(value_rows, gain):
    return value_rows * lax.rsqrt(lax.optimization_barrier(jnp.mean(value_rows * value_rows, -1, keepdims=True)) + EPS) * gain

def causal_conv(value_rows, weight, bias):
    width = weight.shape[0]
    sequence_length = value_rows.shape[0]
    padded = jnp.concatenate([jnp.zeros((width - 1, value_rows.shape[1]), jnp.float32), value_rows], 0)
    total = jnp.zeros_like(value_rows) + bias[None, :]
    for shift in range(width):
        total = total + weight[shift][None, :] * padded[shift:shift + sequence_length]
    return total

def conv_act(value_rows, weight, bias):
    return jax.nn.silu(causal_conv(value_rows, weight, bias))

def state_scan(heads_in, delta, rate, in_map, out_map):
    sequence_length, heads, width = heads_in.shape
    count = sequence_length // CH
    blocks = (heads_in.reshape(count, CH, heads, width), delta.reshape(count, CH, heads), in_map.reshape(count, CH, -1), out_map.reshape(count, CH, -1))
    lower = (jnp.arange(CH)[:, None] >= jnp.arange(CH)[None, :])[:, :, None]

    def advance(state, block):
        x_blk, d_blk, b_blk, c_blk = block
        cum = jnp.cumsum(d_blk * rate[None, :], 0)
        diff = jnp.where(lower, cum[:, None, :] - cum[None, :, :], 0.0)
        decay = jnp.where(lower, jnp.exp(diff), 0.0)
        inner = jnp.dot(c_blk, b_blk.T, precision=HIGH)
        weights = inner[:, :, None] * decay * d_blk[None, :, :]
        local = jnp.einsum('ijh,jhp->ihp', weights, x_blk, precision=HIGH)
        carried = jnp.exp(cum)[:, :, None] * jnp.einsum('in,hpn->ihp', c_blk, state, precision=HIGH)
        tail = jnp.exp(cum[-1][None, :] - cum) * d_blk
        update = jnp.einsum('jhp,jn->hpn', tail[:, :, None] * x_blk, b_blk, precision=HIGH)
        return (jnp.exp(cum[-1])[:, None, None] * state + update, local + carried)
    start = jnp.zeros((heads, width, in_map.shape[1]), jnp.float32)
    _, outs = lax.scan(advance, start, blocks)
    return outs.reshape(sequence_length, heads, width)

def scan_part(value_act, step_pre, step_bias, decay_log, skip_gain, in_map, out_map):
    sequence_length = value_act.shape[0]
    heads = step_pre.shape[1]
    heads_in = value_act.reshape(sequence_length, heads, -1)
    delta = jax.nn.softplus(step_pre + step_bias[None, :])
    rate = -jnp.exp(decay_log)
    outs = state_scan(heads_in, delta, rate, in_map, out_map) + skip_gain[None, :, None] * heads_in
    return outs.reshape(sequence_length, -1)

def expert_plan(routes, count, cap):
    flat = routes.reshape(-1)
    table = (flat[:, None] == jnp.arange(count, dtype=jnp.int32)[None, :]).astype(jnp.int32)
    before = lax.optimization_barrier(jnp.sum((jnp.cumsum(table, 0) - table) * table, 1))
    slot = flat * cap + before
    order = jnp.arange(flat.shape[0], dtype=jnp.int32)
    source = jnp.zeros((count * cap,), jnp.int32).at[slot].set(order)
    filled = jnp.zeros((count * cap,), jnp.int32).at[slot].set(1)
    return (slot, source, filled > 0)

def mixer(rows, params):
    in_gate, in_value, in_state, in_step, mix_output, norm_mix, gated_norm, conv_value_weight, conv_value_bias, conv_state_weight, conv_state_bias, step_bias, decay_log, skip_gain = params
    normalized_input = reduced_input(rms_norm(rows, norm_mix))
    gate_pre = reduced_gradient(score_product(normalized_input, in_gate))
    value_pre = reduced_gradient(score_product(normalized_input, in_value))
    state_pre = reduced_gradient(score_product(normalized_input, in_state))
    step_pre = reduced_gradient(score_product(normalized_input, in_step))
    value_act = conv_act(value_pre, conv_value_weight, conv_value_bias)
    state_act = reduced_input(conv_act(state_pre, conv_state_weight, conv_state_bias))
    ssm_out = scan_part(value_act, step_pre, step_bias, decay_log, skip_gain, state_act[:, :NS], state_act[:, NS:])
    gated = ssm_out * jax.nn.silu(gate_pre)
    mixed = reduced_input(rms_norm(gated, gated_norm))
    return rows + reduced_gradient(score_product(mixed, mix_output))

def experts_layer(rows, params, routes):
    gain, router, gate_w, up_w, down_w, shared_gate, shared_up, shared_down = params
    normalized_input = reduced_input(rms_norm(rows, gain))
    logits = reduced_gradient(score_product(normalized_input, router))
    picked = routes[:, :, None] == jnp.arange(EXPERTS, dtype=jnp.int32)[None, None, :]
    chosen = lax.optimization_barrier(jnp.sum(jnp.where(picked, logits[:, None, :], 0.0), -1))
    gates = jax.nn.softmax(chosen, -1)
    slot, source, filled = expert_plan(routes, EXPERTS, CAP)
    taken = jnp.where(filled[:, None], normalized_input[source // TOP], 0.0).reshape(EXPERTS, CAP, MODEL_WIDTH)
    first = reduced_gradient(jnp.einsum('ecd,edf->ecf', taken, gate_w, precision=HIGH))
    latter_half = reduced_gradient(jnp.einsum('ecd,edf->ecf', taken, up_w, precision=HIGH))
    hidden = reduced_input(jax.nn.silu(first) * latter_half)
    results = reduced_gradient(jnp.einsum('ecf,efd->ecd', hidden, down_w, precision=HIGH)).reshape(EXPERTS * CAP, MODEL_WIDTH)
    routed = results[slot].reshape(rows.shape[0], TOP, MODEL_WIDTH)
    shared_a = reduced_gradient(score_product(normalized_input, shared_gate))
    shared_b = reduced_gradient(score_product(normalized_input, shared_up))
    shared_h = reduced_input(jax.nn.silu(shared_a) * shared_b)
    total = score_product(shared_h, shared_down) + lax.optimization_barrier(jnp.sum(gates[:, :, None] * routed, 1))
    return rows + reduced_gradient(total)

def attention(rows, params):
    gain, query_weight, key_weight, value_weight, w_output = params
    normalized_input = reduced_input(rms_norm(rows, gain))
    sequence_length = rows.shape[0]
    query_groups = QUERY_HEADS // KEY_VALUE_HEADS
    query_rows = reduced_input(reduced_gradient(score_product(normalized_input, query_weight))).reshape(sequence_length, KEY_VALUE_HEADS, query_groups, HEAD_SIZE)
    key_rows = reduced_input(reduced_gradient(score_product(normalized_input, key_weight))).reshape(sequence_length, KEY_VALUE_HEADS, HEAD_SIZE)
    value_rows = reduced_input(reduced_gradient(score_product(normalized_input, value_weight))).reshape(sequence_length, KEY_VALUE_HEADS, HEAD_SIZE)
    scores = reduced_gradient(jnp.einsum('ikgd,jkd->kgij', query_rows, key_rows, precision=HIGH) * HEAD_SIZE ** (-0.5))
    causal = jnp.arange(sequence_length)[:, None] >= jnp.arange(sequence_length)[None, :]
    scores = jnp.where(causal, scores, -1e+30)
    probs = reduced_input(jax.nn.softmax(scores, -1))
    attended = jnp.einsum('kgij,jkd->ikgd', probs, value_rows, precision=HIGH).reshape(sequence_length, QUERY_HEADS * HEAD_SIZE)
    attended = reduced_input(reduced_gradient(attended))
    return rows + reduced_gradient(score_product(attended, w_output))

def block(rows, params, first_routes, second_routes):
    in_gate, in_value, in_state, in_step, mix_output, attn_query, attention_key_matrix, attention_value_matrix, attn_output, shared_gate_one, shared_up_one, shared_down_one, shared_gate_two, shared_up_two, shared_down_two, expert_gate_one, expert_up_one, expert_down_one, expert_gate_two, expert_up_two, expert_down_two, router_one, router_two, norm_mix, norm_moe_one, norm_attn, norm_moe_two, gated_norm, conv_value_weight, conv_value_bias, conv_state_weight, conv_state_bias, step_bias, decay_log, skip_gain = params
    state = mixer(rows, (in_gate, in_value, in_state, in_step, mix_output, norm_mix, gated_norm, conv_value_weight, conv_value_bias, conv_state_weight, conv_state_bias, step_bias, decay_log, skip_gain))
    state = experts_layer(state, (norm_moe_one, router_one, expert_gate_one, expert_up_one, expert_down_one, shared_gate_one, shared_up_one, shared_down_one), first_routes)
    state = attention(state, (norm_attn, attn_query, attention_key_matrix, attention_value_matrix, attn_output))
    state = experts_layer(state, (norm_moe_two, router_two, expert_gate_two, expert_up_two, expert_down_two, shared_gate_two, shared_up_two, shared_down_two), second_routes)
    return state

def reference(hidden_in, out_grad, routes_first, routes_second, in_gate, in_value, in_state, in_step, mix_output, attn_query, attention_key_matrix, attention_value_matrix, attn_output, shared_gate_one, shared_up_one, shared_down_one, shared_gate_two, shared_up_two, shared_down_two, expert_gate_one, expert_up_one, expert_down_one, expert_gate_two, expert_up_two, expert_down_two, router_one, router_two, norm_mix, norm_moe_one, norm_attn, norm_moe_two, gated_norm, conv_value_weight, conv_value_bias, conv_state_weight, conv_state_bias, step_bias, decay_log, skip_gain):
    weights = (in_gate, in_value, in_state, in_step, mix_output, attn_query, attention_key_matrix, attention_value_matrix, attn_output, shared_gate_one, shared_up_one, shared_down_one, shared_gate_two, shared_up_two, shared_down_two, expert_gate_one, expert_up_one, expert_down_one, expert_gate_two, expert_up_two, expert_down_two, router_one, router_two, norm_mix, norm_moe_one, norm_attn, norm_moe_two, gated_norm, conv_value_weight, conv_value_bias, conv_state_weight, conv_state_bias, step_bias, decay_log, skip_gain)
    weights = tuple((item.astype(jnp.float32) for item in weights))
    first_all = routes_first.reshape(N_DP, LEN, TOP)
    second_all = routes_second.reshape(N_DP, LEN, TOP)

    def forward(inputs, params):

        def advance(carry, item):
            rows, first, latter_half = item

            def single(value_rows, kept):
                return block(value_rows, kept, first, latter_half)
            return (carry, jax.checkpoint(single)(rows, params))
        _, outs = lax.scan(advance, 0, (inputs.reshape(N_DP, LEN, MODEL_WIDTH), first_all, second_all))
        return outs.reshape(N_DP * LEN, MODEL_WIDTH)
    outputs, pull = jax.vjp(forward, hidden_in.astype(jnp.float32), weights)
    grad_in, grads = pull(out_grad.astype(jnp.float32))
    return (outputs, grad_in, grads[0], grads[1], grads[2], grads[3], grads[4], grads[5], grads[6], grads[7], grads[8], grads[9], grads[10], grads[11], grads[12], grads[13], grads[14], grads[15], grads[16], grads[17], grads[18], grads[19], grads[20], grads[21], grads[22], grads[23], grads[24], grads[25], grads[26], grads[27], grads[28], grads[29], grads[30], grads[31], grads[32], grads[33], grads[34])
```

```python
import jax
import jax.numpy as jnp
from jax import lax
from jax.sharding import PartitionSpec as P

MH = 48
NS = 128
CH = 128
QUERY_HEADS = 12
KEY_VALUE_HEADS = 4
HEAD_SIZE = 128
TOP = 6
LEN = 256
DI = 3072


EPS = 1e-05
HIGH = lax.Precision.HIGHEST


def matmul(left, right):
    return jnp.dot(left, right, preferred_element_type=jnp.float32)


def times_back(left, right):
    return lax.dot_general(
        left, right, (((1,), (1,)), ((), ())), preferred_element_type=jnp.float32
    )


def times_over(left, right):
    return lax.dot_general(
        left, right, (((0,), (0,)), ((), ())), preferred_element_type=jnp.float32
    )


def rms_norm(value_rows, gain):
    return value_rows * lax.rsqrt(jnp.mean(value_rows * value_rows, -1, keepdims=True) + EPS) * gain


def causal_conv(value_rows, weight, bias):
    width = weight.shape[0]
    sequence_length = value_rows.shape[0]
    padded = jnp.concatenate(
        [jnp.zeros((width - 1, value_rows.shape[1]), jnp.float32), value_rows], 0
    )
    total = jnp.zeros_like(value_rows) + bias[None, :]
    for shift in range(width):
        total = total + weight[shift][None, :] * padded[shift : shift + sequence_length]
    return total


def conv_act(value_rows, weight, bias):
    return jax.nn.silu(causal_conv(value_rows, weight, bias))


def state_scan(heads_in, delta, rate, in_map, out_map):
    sequence_length, heads, width = heads_in.shape
    count = sequence_length // CH
    blocks = (
        heads_in.reshape(count, CH, heads, width),
        delta.reshape(count, CH, heads),
        in_map.reshape(count, CH, -1),
        out_map.reshape(count, CH, -1),
    )
    lower = (jnp.arange(CH)[:, None] >= jnp.arange(CH)[None, :])[:, :, None]

    def advance(state, block):
        x_blk, d_blk, b_blk, c_blk = block
        cum = jnp.cumsum(d_blk * rate[None, :], 0)
        diff = jnp.where(lower, cum[:, None, :] - cum[None, :, :], 0.0)
        decay = jnp.where(lower, jnp.exp(diff), 0.0)
        inner = jnp.dot(c_blk, b_blk.T, precision=HIGH)
        weights = inner[:, :, None] * decay * d_blk[None, :, :]
        local = jnp.einsum("ijh,jhp->ihp", weights, x_blk, precision=HIGH)
        carried = jnp.exp(cum)[:, :, None] * jnp.einsum("in,hpn->ihp", c_blk, state, precision=HIGH)
        tail = jnp.exp(cum[-1][None, :] - cum) * d_blk
        update = jnp.einsum("jhp,jn->hpn", tail[:, :, None] * x_blk, b_blk, precision=HIGH)
        return (jnp.exp(cum[-1])[:, None, None] * state + update, local + carried)

    start = jnp.zeros((heads, width, in_map.shape[1]), jnp.float32)
    outs, state = [], start
    for at in range(count):
        state, out = advance(state, tuple(block[at] for block in blocks))
        outs.append(out)
    return jnp.concatenate(outs, 0)


def scan_part(value_act, step_pre, step_bias, decay_log, skip_gain, in_map, out_map):
    sequence_length = value_act.shape[0]
    heads = step_pre.shape[1]
    heads_in = value_act.reshape(sequence_length, heads, -1)
    delta = jax.nn.softplus(step_pre + step_bias[None, :])
    rate = -jnp.exp(decay_log)
    outs = state_scan(heads_in, delta, rate, in_map, out_map) + skip_gain[None, :, None] * heads_in
    return outs.reshape(sequence_length, -1)


def silu_slope(value_rows):
    sig = jax.nn.sigmoid(value_rows)
    return sig * (1.0 + value_rows * (1.0 - sig))


AXES = ("dp", "tensor")
SPARE = 128
MOST_ROWS = 4096


def total_of(left, right):
    return left.astype(jnp.float32) + right.astype(jnp.float32)


def low(value_rows):
    return value_rows.astype(jnp.bfloat16)


def together(values):
    return lax.optimization_barrier(values)


def after(value, *others):
    return lax.optimization_barrier((value, others))[0]


class Grid:
    def __init__(self):
        self.dp = lax.axis_size("dp")
        self.nt = lax.axis_size("tensor")
        self.nc = 2
        self.na = 4
        self.nb = self.dp // (self.na * self.nc)
        index = lax.axis_index("dp")
        self.index = index
        self.c = index % self.nc
        self.b = (index // self.nc) % self.nb
        self.a = index // (self.nc * self.nb)
        self.t = lax.axis_index("tensor")
        self.step_t = (1, self.nt)
        self.step_c = (self.nt, self.nc)
        self.step_b = (self.nt * self.nc, self.nb)
        self.step_a = (self.nt * self.nc * self.nb, self.na)

    def shift(self, value, step, amount):
        stride, size = step
        pairs = []
        for source in range(self.dp * self.nt):
            digit = (source // stride) % size
            pairs.append((source, source + ((digit + amount) % size - digit) * stride))
        return lax.ppermute(value, AXES, pairs)

    def around(self, value, step):
        held = [value]
        for _ in range(step[1] - 1):
            held.append(self.shift(held[-1], step, 1))
        return held

    def sum_around(self, part, step):
        size = step[1]
        held = part(size - 1)
        for k in range(size - 2, -1, -1):
            held = total_of(part(k), self.shift(low(held), step, -1))
        return held

    def rounds(self, value):
        for k in range(self.na):
            ahead = self.shift(value, self.step_a, 1) if k < self.na - 1 else None
            near = self.around(value, self.step_b)
            if ahead is not None:
                ahead, near = together((ahead, near))
            yield near
            value = ahead

    def nearby(self):
        return [
            [
                (((self.a - k) % self.na) * self.nb + (self.b - kb) % self.nb) * self.nc
                + (self.c - kc) % self.nc
                for kc in range(self.nc)
                for kb in range(self.nb)
            ]
            for k in range(self.na)
        ]

    def with_core(self, near):
        return jnp.concatenate(near + [self.shift(block, self.step_c, 1) for block in near], 0)

    def core_sum(self, value):
        half = value.shape[0] // 2
        return low(total_of(value[:half], self.shift(value[half:], self.step_c, 1)))

    def collect_rounds(self, parts):
        total = None
        for k in range(self.na - 1, -1, -1):
            part = parts[k]
            count = part.shape[0] // self.nb
            if total is not None:
                part, total = together((part, low(total)))
                moved = self.shift(total, self.step_a, -1)
            near = self.sum_around(lambda kb: part[kb * count : (kb + 1) * count], self.step_b)
            if total is not None:
                near, moved = together((near, moved))
                near = total_of(near, moved)
            total = near
        return total

    def in_turn(self, step, value, rest, collect=None):
        if self.dp * value.shape[0] > MOST_ROWS:

            def near_of(held):
                return self.around(held, self.step_b)

            def advance(carry, item):
                held, total = carry
                part, *others = step(near_of(held), item)
                if collect is not None:
                    total = [old + new for old, new in zip(total, collect(item, others))]
                    others = []
                return (self.shift(held, self.step_a, 1), total), (part, others)

            total = []
            if collect is not None:
                item = tuple(leaf[0] for leaf in rest)
                shapes = jax.eval_shape(
                    lambda *args: collect(args[1], step(near_of(args[0]), args[1])[1:]), value, item
                )
                total = [jnp.zeros(shape.shape, jnp.float32) for shape in shapes]
            (_, total), (parts, others) = lax.scan(advance, (value, total), rest)
            others = others if collect is None else total
        else:
            results = [
                step(near, tuple(leaf[k] for leaf in rest))
                for k, near in enumerate(self.rounds(value))
            ]
            parts, *others = [list(leaves) for leaves in zip(*results)]
            if collect is not None:
                rows = [jnp.concatenate(list(leaf), 0) for leaf in rest]
                others = collect(rows, [jnp.concatenate(leaf, 0) for leaf in others])
        return self.collect_rounds(parts), others

    def gather_weight(self, value):
        held = []
        for near in self.rounds(value):
            held.extend(near)
        return self.with_core(held)

    def order(self, rows):
        at = jnp.arange(self.dp * rows, dtype=jnp.int32)
        kc, ka, kb = (
            at // (rows * self.nb * self.na),
            (at // (rows * self.nb)) % self.na,
            (at // rows) % self.nb,
        )
        a, b, c = (self.a - ka) % self.na, (self.b - kb) % self.nb, (self.c - kc) % self.nc
        source = ((a * self.nb + b) * self.nc + c) * rows + at % rows
        return low(jnp.arange(self.dp * rows, dtype=jnp.int32)[:, None] == source[None, :])

    def all_sum(self, value):
        half = value.shape[0] // 2
        keep = lax.dynamic_slice_in_dim(value, self.c * half, half, 0)
        send = lax.dynamic_slice_in_dim(value, (1 - self.c) * half, half, 0)
        value = keep + self.shift(send, self.step_c, 1)
        for step in (self.step_t, self.step_b, self.step_a):
            value = sum(self.around(value, step))
        other = self.shift(value, self.step_c, 1)
        return jnp.where(
            self.c == 0,
            jnp.concatenate([value, other], 0),
            jnp.concatenate([other, value], 0),
        )

    def scatter_weight(self, value):
        rows = value.shape[0] // self.dp
        parts = value.reshape(self.na * self.nb, self.nc, rows, -1)
        send = lax.dynamic_index_in_dim(parts, (self.c + 1) % self.nc, 1, keepdims=False)
        keep = lax.dynamic_index_in_dim(parts, self.c, 1, keepdims=False)
        both = low(total_of(keep, self.shift(send, self.step_c, 1)))

        def block(ka, kb):
            at = ((self.a - ka) % self.na) * self.nb + (self.b - kb) % self.nb
            return lax.dynamic_index_in_dim(both, at, 0, keepdims=False)

        return self.collect_rounds(
            [
                jnp.concatenate([block(ka, kb) for kb in range(self.nb)], 0)
                for ka in range(self.na)
            ]
        )

    def swap(self, value):
        return self.shift(value, self.step_t, 1)

    def pair_rows(self, value):
        other = self.swap(value)
        return jnp.where(
            self.t == 0,
            jnp.concatenate([value, other], 0),
            jnp.concatenate([other, value], 0),
        )

    def pair_sum(self, value, axis):
        half = value.shape[axis] // 2
        keep = lax.dynamic_slice_in_dim(value, self.t * half, half, axis)
        send = lax.dynamic_slice_in_dim(value, (1 - self.t) * half, half, axis)
        return total_of(keep, self.swap(low(send)))


def dense_gates(logits, picked):
    shown = jnp.where(picked, logits, -1e30)
    raised = jnp.where(picked, jnp.exp(logits - jnp.max(shown, 1, keepdims=True)), 0.0)
    return raised / jnp.sum(raised, 1, keepdims=True)


def body(
    hidden_in,
    out_grad,
    routes_first,
    routes_second,
    in_gate,
    in_value,
    in_state,
    in_step,
    mix_output,
    attn_query,
    attention_key_matrix,
    attention_value_matrix,
    attn_output,
    shared_gate_one,
    shared_up_one,
    shared_down_one,
    shared_gate_two,
    shared_up_two,
    shared_down_two,
    expert_gate_one,
    expert_up_one,
    expert_down_one,
    expert_gate_two,
    expert_up_two,
    expert_down_two,
    router_one,
    router_two,
    norm_mix,
    norm_moe_one,
    norm_attn,
    norm_moe_two,
    gated_norm,
    conv_value_weight,
    conv_value_bias,
    conv_state_weight,
    conv_state_bias,
    step_bias,
    decay_log,
    skip_gain,
):
    grid = Grid()
    tensor_rank = grid.t
    expert_count = grid.dp
    local_rows = hidden_in.shape[0]
    value_cols = in_value.shape[1]
    state_cols = in_state.shape[1]
    head_cols = in_step.shape[1]
    value_start = tensor_rank * value_cols
    state_start = tensor_rank * state_cols
    head_start = tensor_rank * head_cols
    norm_local = lax.dynamic_slice_in_dim(gated_norm, value_start, value_cols, 0)
    value_kernel = lax.dynamic_slice_in_dim(conv_value_weight, value_start, value_cols, 1)
    value_offset = lax.dynamic_slice_in_dim(conv_value_bias, value_start, value_cols, 0)
    state_kernel = lax.dynamic_slice_in_dim(conv_state_weight, state_start, state_cols, 1)
    state_offset = lax.dynamic_slice_in_dim(conv_state_bias, state_start, state_cols, 0)
    bias_local = lax.dynamic_slice_in_dim(step_bias, head_start, head_cols, 0)
    decay_local = lax.dynamic_slice_in_dim(decay_log, head_start, head_cols, 0)
    skip_local = lax.dynamic_slice_in_dim(skip_gain, head_start, head_cols, 0)
    scale = HEAD_SIZE ** (-0.5)
    model = hidden_in.shape[1]
    narrow = state_cols + head_cols
    block_rows = in_value.shape[0]

    rows = hidden_in.astype(jnp.float32)
    normalized_input, norm_pull = jax.vjp(rms_norm, rows, norm_mix)
    full = grid.pair_rows(low(normalized_input))
    sequence_length = full.shape[0]
    order = grid.order(block_rows)

    w_first = grid.gather_weight(
        jnp.concatenate(
            [in_value, in_state, in_step, jnp.zeros((block_rows, -narrow % 128), jnp.bfloat16)], 1
        )
    )
    value_weight = w_first[:, :value_cols]
    w_narrow = w_first[:, value_cols:]
    w_gate = grid.gather_weight(after(in_gate, w_first))
    w_out_t = grid.gather_weight(after(mix_output.T, w_gate))
    q_cols = attn_query.shape[1]
    k_cols = attention_key_matrix.shape[1]
    wide_cols = q_cols + 2 * k_cols

    shared_units = shared_gate_one.shape[1] // expert_count
    shared_parts = jnp.stack(
        [
            shared_gate_one,
            shared_up_one,
            shared_down_one.T,
            shared_gate_two,
            shared_up_two,
            shared_down_two.T,
        ],
        1,
    ).reshape(block_rows, 6, expert_count, shared_units)
    shared_parts = shared_parts.transpose(2, 0, 1, 3)
    shared_own = lax.all_to_all(
        after(shared_parts.reshape(expert_count, block_rows, 6 * shared_units), w_first),
        "dp",
        split_axis=0,
        concat_axis=0,
        tiled=True,
    ).reshape(model, 6 * shared_units)
    shared_other = grid.swap(shared_own)

    def shared_of(which):
        at = which * shared_units
        return [
            shared_own[:, at : at + shared_units],
            shared_other[:, at : at + shared_units],
        ]

    def expert_weights(bank, which, when):
        own = [leaf[0] for leaf in bank]
        gate_other, up_other, down_other = [grid.swap(leaf) for leaf in after(own, when)]
        gate_own, up_own, down_own = own
        w_in = jnp.concatenate(
            [gate_own, gate_other, up_own, up_other] + shared_of(which) + shared_of(which + 1), 1
        )
        down_t = jnp.concatenate(shared_of(which + 2), 1)
        w_down = jnp.concatenate([down_own, down_other, down_t.T], 0)
        return w_in, w_down

    experts_one = expert_weights((expert_gate_one, expert_up_one, expert_down_one), 0, full)
    half_units = expert_gate_one.shape[2]
    units = 2 * half_units
    pair_units = 2 * shared_units

    def local_mask(routes):
        mine = lax.dynamic_slice_in_dim(routes, tensor_rank * local_rows, local_rows, 0)
        names = jnp.arange(expert_count, dtype=jnp.int32)
        return jnp.any(mine[:, :, None] == names[None, None, :], 1)

    mask_one, mask_two = local_mask(routes_first), local_mask(routes_second)
    masks = lax.all_gather(low(jnp.concatenate([mask_one, mask_two], 1)), "dp", axis=0)
    masks = [
        jnp.concatenate([masks[at] for at in blocks], 0) > 0.5 for blocks in grid.nearby()
    ]
    picked_one = jnp.stack([mask[:, :expert_count] for mask in masks])
    picked_two = jnp.stack([mask[:, expert_count:] for mask in masks])
    here = (jnp.arange(expert_count, dtype=jnp.int32) == grid.index)[None, :]

    def split_up(before):
        wide = before.astype(jnp.float32)
        edges = [units, 2 * units, 2 * units + pair_units]
        return jnp.split(wide, edges, 1)

    def moe_forward(rows, gain, router, picked, weights):
        w_in, w_down = weights
        normalized_input, norm_pull = jax.vjp(rms_norm, rows, gain)
        local = low(normalized_input)

        def step(near, chunk):
            (chosen,) = chunk
            every = grid.with_core(near)
            gates = dense_gates(matmul(every, router), chosen)
            gate = jnp.sum(jnp.where(here, gates, 0.0), 1, keepdims=True)
            before = low(matmul(every, w_in))
            first, second, shared_a, shared_b = split_up(before)
            hidden = jnp.concatenate(
                [
                    low(jax.nn.silu(first) * second * gate),
                    low(jax.nn.silu(shared_a) * shared_b),
                ],
                1,
            )
            part = grid.core_sum(low(matmul(hidden, w_down)))
            return (part, every, gate, before, hidden)

        result, kept = grid.in_turn(step, local, (picked,))
        return (rows + result, (norm_pull, local, kept))

    def moe_backward(grad, router, local_picked, weights, keep):
        w_in, w_down = weights
        norm_pull, local, kept = keep
        spare = jnp.arange(SPARE, dtype=jnp.int32)[None, :] == grid.index

        def step(near, chunk):
            _, gate, before, _ = chunk
            d_every = grid.with_core(near)
            first, second, shared_a, shared_b = split_up(before)
            d_before = low(times_back(d_every, w_down)).astype(jnp.float32)
            d_hidden, d_shared = d_before[:, :units], d_before[:, units:]
            active = jax.nn.silu(first)
            d_gate = jnp.sum(d_hidden * active * second, 1, keepdims=True)
            d_hidden = d_hidden * gate
            d_in = jnp.concatenate(
                [
                    low(d_hidden * second * silu_slope(first)),
                    low(d_hidden * active),
                    low(d_shared * shared_b * silu_slope(shared_a)),
                    low(d_shared * jax.nn.silu(shared_a)),
                ],
                1,
            )
            d_in = together(d_in)
            sent = jnp.concatenate(
                [low(times_back(d_in, w_in)), low(jnp.where(spare, d_gate, 0.0))], 1
            )
            return (grid.core_sum(sent), d_every, d_in)

        def collect(chunk, more):
            every, _, _, hidden = chunk
            d_every, d_in = more
            return times_over(every, d_in), times_over(hidden, d_every)

        got, (g_in, g_down) = grid.in_turn(step, low(grad), kept, collect)
        own, other = slice(0, half_units), slice(half_units, units)
        own_up = slice(units, units + half_units)
        other_up = slice(units + half_units, 2 * units)
        g_experts = (
            (g_in[:, own] + grid.swap(low(g_in[:, other])))[None],
            (g_in[:, own_up] + grid.swap(low(g_in[:, other_up])))[None],
            (g_down[own] + grid.swap(low(g_down[other])))[None],
        )
        g_rest, g_rest_down = g_in[:, 2 * units :], g_down[units:].T
        s = shared_units
        mine = jnp.concatenate([g_rest[:, :s], g_rest[:, 2 * s : 3 * s], g_rest_down[:, :s]], 1)
        theirs = jnp.concatenate([g_rest[:, s : 2 * s], g_rest[:, 3 * s :], g_rest_down[:, s:]], 1)
        g_shared = low(mine + grid.swap(low(theirs)))
        gates = dense_gates(matmul(local, router), local_picked)
        d_gates = got[:, model : model + expert_count]
        d_logits = low(gates * (d_gates - jnp.sum(gates * d_gates, 1, keepdims=True)))
        d_local = got[:, :model] + times_back(d_logits, router)
        g_router = times_over(d_logits, local)
        d_rows, g_gain = norm_pull(d_local)
        return (grad + d_rows, g_gain, g_router, g_shared, g_experts)

    ordered = low(matmul(full, order))
    value_pre = matmul(ordered, value_weight)
    narrow_pre = matmul(ordered, w_narrow)
    state_pre = narrow_pre[:, :state_cols]
    step_pre = narrow_pre[:, state_cols:narrow]
    gate_pre = matmul(ordered, w_gate)
    value_act, value_pull = jax.vjp(conv_act, value_pre, value_kernel, value_offset)
    state_act, state_pull = jax.vjp(conv_act, state_pre, state_kernel, state_offset)
    state_own = low(state_act)
    state_other = grid.swap(state_own)
    in_map = jnp.where(tensor_rank == 0, state_own, state_other).astype(jnp.float32)
    out_map = jnp.where(tensor_rank == 0, state_other, state_own).astype(jnp.float32)
    ssm_out, scan_pull = jax.vjp(
        scan_part, value_act, step_pre, bias_local, decay_local, skip_local, in_map, out_map
    )
    gated = ssm_out * jax.nn.silu(gate_pre)
    square = jnp.sum(gated * gated, 1, keepdims=True)
    inverse = lax.rsqrt((square + grid.swap(square)) / DI + EPS)
    mixed = low(gated * inverse * norm_local)
    mixed_out = low(times_back(low(times_back(mixed, w_out_t)), order))
    result = rows + grid.pair_sum(mixed_out, 0)
    experts_two = expert_weights((expert_gate_two, expert_up_two, expert_down_two), 3, result)
    w_attention = lax.all_gather(
        after(
            jnp.concatenate(
                [attn_query, attention_key_matrix, attention_value_matrix, attn_output.T], 1
            ),
            w_out_t,
        ),
        "dp",
        axis=0,
        tiled=True,
    )
    qkv_weight = w_attention[:, :wide_cols]
    attn_out_t = w_attention[:, wide_cols:]
    state_two, moe_one_keep = moe_forward(result, norm_moe_one, router_one, picked_one, experts_one)

    normalized_input, attention_norm_pull = jax.vjp(rms_norm, state_two, norm_attn)
    attention_full = grid.pair_rows(low(normalized_input))
    kv_heads = k_cols // HEAD_SIZE
    query_groups = QUERY_HEADS // KEY_VALUE_HEADS
    qkv = low(matmul(attention_full, qkv_weight))
    query_rows = qkv[:, :q_cols].reshape(sequence_length, kv_heads, query_groups, HEAD_SIZE)
    key_rows = qkv[:, q_cols : q_cols + k_cols].reshape(sequence_length, kv_heads, HEAD_SIZE)
    value_rows = qkv[:, q_cols + k_cols :].reshape(sequence_length, kv_heads, HEAD_SIZE)
    causal = jnp.arange(sequence_length)[:, None] >= jnp.arange(sequence_length)[None, :]
    scores = (
        jnp.einsum("ikgd,jkd->kgij", query_rows, key_rows, preferred_element_type=jnp.float32)
        * scale
    )
    scores = jnp.where(causal, scores, -1e30)
    peak = jnp.max(scores, 3, keepdims=True)
    raised = jnp.exp(scores - peak)
    total = jnp.sum(raised, 3, keepdims=True)
    probs = raised / total
    low_probs = low(probs)
    attended = jnp.einsum(
        "kgij,jkd->ikgd", low_probs, value_rows, preferred_element_type=jnp.float32
    )
    attended = low(attended.reshape(sequence_length, -1))
    result = state_two + grid.pair_sum(times_back(attended, attn_out_t), 0)
    block_out, moe_two_keep = moe_forward(
        result, norm_moe_two, router_two, picked_two, experts_two
    )

    grad = out_grad.astype(jnp.float32)
    grad, g_nmoe_two, g_router_two, g_shared_two, g_experts_two = moe_backward(
        grad, router_two, mask_two, experts_two, moe_two_keep
    )

    dfull = grid.pair_rows(low(grad))
    d_att = low(matmul(dfull, attn_out_t)).reshape(query_rows.shape)
    g_out_t = low(times_over(dfull, attended))
    d_probs = jnp.einsum("ikgd,jkd->kgij", d_att, value_rows, preferred_element_type=jnp.float32)
    d_scores = low(probs * (d_probs - jnp.sum(probs * d_probs, 3, keepdims=True)))
    d_query = low(
        jnp.einsum("kgij,jkd->ikgd", d_scores, key_rows, preferred_element_type=jnp.float32) * scale
    ).reshape(sequence_length, -1)
    d_keys = low(
        jnp.einsum("kgij,ikgd->jkd", d_scores, query_rows, preferred_element_type=jnp.float32)
        * scale
    ).reshape(sequence_length, -1)
    d_values = low(
        jnp.einsum("kgij,ikgd->jkd", low_probs, d_att, preferred_element_type=jnp.float32)
    ).reshape(sequence_length, -1)
    d_qkv = jnp.concatenate([d_query, d_keys, d_values], 1)
    g_qkv = low(times_over(attention_full, d_qkv))
    d_rows, g_nattn = attention_norm_pull(grid.pair_sum(times_back(d_qkv, qkv_weight), 0))
    grad = grad + d_rows

    grad, g_nmoe_one, g_router_one, g_shared_one, g_experts_one = moe_backward(
        grad, router_one, mask_one, experts_one, moe_one_keep
    )

    attention_sum = grid.scatter_weight(after(jnp.concatenate([g_qkv, g_out_t], 1), grad))
    dfull = grid.pair_rows(low(grad))
    d_mixed = matmul(low(matmul(dfull, order)), w_out_t)
    mix_out_sum = grid.scatter_weight(after(low(times_over(dfull, mixed)), attention_sum))
    weighted = d_mixed * norm_local
    total = jnp.sum(weighted * gated, 1, keepdims=True)
    total = total + grid.swap(total)
    d_gated = weighted * inverse - gated * inverse**3 * (total / DI)
    g_ngated = jnp.sum(d_mixed * gated * inverse, 0)
    d_ssm = d_gated * jax.nn.silu(gate_pre)
    low_gate = low(d_gated * ssm_out * silu_slope(gate_pre))
    gate_sum = grid.scatter_weight(after(low(times_over(full, low_gate)), mix_out_sum))
    d_ssm = after(d_ssm, attention_sum)
    d_value_act, d_step, g_bias, g_decay, g_skip, d_in_map, d_out_map = scan_pull(d_ssm)
    map_keep = jnp.where(tensor_rank == 0, d_in_map, d_out_map)
    map_send = jnp.where(tensor_rank == 0, d_out_map, d_in_map)
    d_state_act = total_of(map_keep, grid.swap(low(map_send)))
    d_value, g_vkernel, g_voffset = value_pull(d_value_act)
    d_state, g_skernel, g_soffset = state_pull(d_state_act)
    low_value = after(low(d_value), gate_sum)
    low_narrow = jnp.concatenate(
        [low(d_state), low(d_step), jnp.zeros((sequence_length, -narrow % 128), jnp.bfloat16)], 1
    )
    d_normed = (
        times_back(low_gate, w_gate)
        + times_back(low_value, value_weight)
        + times_back(low_narrow, w_narrow)
    )
    value_sum = grid.scatter_weight(
        low(jnp.concatenate([times_over(full, low_value), times_over(full, low_narrow)], 1))
    )
    d_normed = times_back(low(d_normed), order)
    d_rows, g_nmix = norm_pull(grid.pair_sum(d_normed, 0))
    grad = grad + d_rows

    shared_grads = jnp.concatenate([g_shared_one, g_shared_two], 1)
    shared_back = lax.all_to_all(
        shared_grads.reshape(expert_count, block_rows, 6 * shared_units),
        "dp",
        split_axis=0,
        concat_axis=0,
        tiled=True,
    ).astype(jnp.float32)
    shared_back = shared_back.reshape(expert_count, block_rows, 6, shared_units)
    shared_back = shared_back.transpose(2, 1, 0, 3).reshape(6, block_rows, -1)

    def spread(value, start, whole):
        value = value.reshape(-1, value.shape[-1])
        wide = jnp.zeros((value.shape[0], whole), jnp.float32)
        return lax.dynamic_update_slice_in_dim(wide, value, start, 1).reshape(-1)

    def all_sums(pieces):
        sizes = [piece.size for piece in pieces]
        packed = [piece.reshape(-1) for piece in pieces]
        packed.append(jnp.zeros((-sum(sizes) % 2048,), jnp.float32))
        packed = grid.all_sum(jnp.concatenate(packed).reshape(-1, 128)).reshape(-1)
        summed, at = [], 0
        for size in sizes:
            summed.append(packed[at : at + size])
            at += size
        return summed

    summed = all_sums((g_router_one, g_router_two, g_nmoe_one, g_nattn, g_nmoe_two))
    summed = summed[:2] + all_sums((g_nmix,)) + summed[2:]
    summed += all_sums(
        (
            spread(g_ngated, value_start, DI),
            spread(g_vkernel, value_start, DI),
            spread(g_voffset, value_start, DI),
            spread(g_skernel, state_start, 2 * NS),
            spread(g_soffset, state_start, 2 * NS),
            spread(g_bias, head_start, MH),
            spread(g_decay, head_start, MH),
            spread(g_skip, head_start, MH),
        )
    )
    return (
        block_out,
        grad,
        gate_sum,
        value_sum[:, :value_cols],
        value_sum[:, value_cols : value_cols + state_cols],
        value_sum[:, value_cols + state_cols : value_cols + narrow],
        mix_out_sum.T,
        attention_sum[:, :q_cols],
        attention_sum[:, q_cols : q_cols + k_cols],
        attention_sum[:, q_cols + k_cols : wide_cols],
        attention_sum[:, wide_cols:].T,
        shared_back[0],
        shared_back[1],
        shared_back[2].T,
        shared_back[3],
        shared_back[4],
        shared_back[5].T,
        g_experts_one[0],
        g_experts_one[1],
        g_experts_one[2],
        g_experts_two[0],
        g_experts_two[1],
        g_experts_two[2],
        summed[0].reshape(expert_count, model).T,
        summed[1].reshape(expert_count, model).T,
        summed[2],
        summed[3],
        summed[4],
        summed[5],
        summed[6],
        summed[7].reshape(-1, DI),
        summed[8],
        summed[9].reshape(-1, 2 * NS),
        summed[10],
        summed[11],
        summed[12],
        summed[13],
    )


def solution(mesh):
    in_specs = (
        P(("dp", "tensor"), None),
        P(("dp", "tensor"), None),
        P("dp", None),
        P("dp", None),
        P("dp", "tensor"),
        P("dp", "tensor"),
        P("dp", "tensor"),
        P("dp", "tensor"),
        P("tensor", "dp"),
        P("dp", "tensor"),
        P("dp", "tensor"),
        P("dp", "tensor"),
        P("tensor", "dp"),
        P("dp", "tensor"),
        P("dp", "tensor"),
        P("tensor", "dp"),
        P("dp", "tensor"),
        P("dp", "tensor"),
        P("tensor", "dp"),
        P("dp", None, "tensor"),
        P("dp", None, "tensor"),
        P("dp", "tensor", None),
        P("dp", None, "tensor"),
        P("dp", None, "tensor"),
        P("dp", "tensor", None),
        P(),
        P(),
        P(),
        P(),
        P(),
        P(),
        P(),
        P(),
        P(),
        P(),
        P(),
        P(),
        P(),
        P(),
    )
    out_specs = (
        P(("dp", "tensor"), None),
        P(("dp", "tensor"), None),
        P("dp", "tensor"),
        P("dp", "tensor"),
        P("dp", "tensor"),
        P("dp", "tensor"),
        P("tensor", "dp"),
        P("dp", "tensor"),
        P("dp", "tensor"),
        P("dp", "tensor"),
        P("tensor", "dp"),
        P("dp", "tensor"),
        P("dp", "tensor"),
        P("tensor", "dp"),
        P("dp", "tensor"),
        P("dp", "tensor"),
        P("tensor", "dp"),
        P("dp", None, "tensor"),
        P("dp", None, "tensor"),
        P("dp", "tensor", None),
        P("dp", None, "tensor"),
        P("dp", None, "tensor"),
        P("dp", "tensor", None),
        P(),
        P(),
        P(),
        P(),
        P(),
        P(),
        P(),
        P(),
        P(),
        P(),
        P(),
        P(),
        P(),
        P(),
    )
    return jax.shard_map(body, mesh=mesh, in_specs=in_specs, out_specs=out_specs, check_vma=False)
```

```python
import jax
import jax.numpy as jnp
from jax import lax
from jax.sharding import PartitionSpec as P

MH = 48
NS = 128
CH = 128
QUERY_HEADS = 12
KEY_VALUE_HEADS = 4
HEAD_SIZE = 128
TOP = 6
LEN = 256
DI = 3072


EPS = 1e-05
HIGH = lax.Precision.HIGHEST


def matmul(left, right):
    return jnp.dot(left, right, preferred_element_type=jnp.float32)


def times_back(left, right):
    return lax.dot_general(
        left, right, (((1,), (1,)), ((), ())), preferred_element_type=jnp.float32
    )


def times_over(left, right):
    return lax.dot_general(
        left, right, (((0,), (0,)), ((), ())), preferred_element_type=jnp.float32
    )


def rms_norm(value_rows, gain):
    return value_rows * lax.rsqrt(jnp.mean(value_rows * value_rows, -1, keepdims=True) + EPS) * gain


def causal_conv(value_rows, weight, bias):
    width = weight.shape[0]
    sequence_length = value_rows.shape[0]
    padded = jnp.concatenate(
        [jnp.zeros((width - 1, value_rows.shape[1]), jnp.float32), value_rows], 0
    )
    total = jnp.zeros_like(value_rows) + bias[None, :]
    for shift in range(width):
        total = total + weight[shift][None, :] * padded[shift : shift + sequence_length]
    return total


def conv_act(value_rows, weight, bias):
    return jax.nn.silu(causal_conv(value_rows, weight, bias))


def silu_slope(value_rows):
    sig = jax.nn.sigmoid(value_rows)
    return sig * (1.0 + value_rows * (1.0 - sig))


AXES = ("dp", "tensor")
SPARE = 128
MASK_COLUMNS = 384
SCAN = lax.Precision.DEFAULT
MOST_ROWS = 4096


def scan_block(x_blk, step_blk, step_bias, decay_log, skip_gain, b_blk, c_blk, state, more):
    rows = x_blk.shape[0]
    lower = (jnp.arange(rows)[:, None] >= jnp.arange(rows)[None, :])[:, :, None]
    d_blk = jax.nn.softplus(step_blk + step_bias[None, :])
    cum = jnp.cumsum(d_blk * -jnp.exp(decay_log)[None, :], 0)
    diff = jnp.where(lower, cum[:, None, :] - cum[None, :, :], 0.0)
    decay = jnp.where(lower, jnp.exp(diff), 0.0)
    inner = jnp.dot(c_blk, b_blk.T, precision=SCAN)
    weights = inner[:, :, None] * decay * d_blk[None, :, :]
    out = jnp.einsum("ijh,jhp->ihp", weights, x_blk, precision=SCAN) + skip_gain[None, :, None] * x_blk
    if state is not None:
        out = out + jnp.exp(cum)[:, :, None] * jnp.einsum(
            "in,hpn->ihp", c_blk, state, precision=SCAN
        )
    if not more:
        return None, out
    tail = jnp.exp(cum[-1][None, :] - cum) * d_blk
    update = jnp.einsum("jhp,jn->hpn", tail[:, :, None] * x_blk, b_blk, precision=SCAN)
    if state is not None:
        update = update + jnp.exp(cum[-1])[:, None, None] * state
    return update, out


def total_of(left, right):
    return left.astype(jnp.float32) + right.astype(jnp.float32)


def low(value_rows):
    return value_rows.astype(jnp.bfloat16)


def together(values):
    return lax.optimization_barrier(values)


def after(value, *others):
    return lax.optimization_barrier((value, others))[0]


class Beside:
    def __init__(self, work=None):
        self.work = work
        self.result = None
        self.pending = None
        if work is not None:
            self.advance(None)

    def advance(self, value):
        try:
            self.pending = self.work.send(value)
        except StopIteration as stop:
            self.work, self.result = None, stop.value

    def together(self, held):
        if self.work is None:
            return together(held)
        held, value = together((held, self.pending))
        self.advance(value)
        return held

    def finish(self):
        while self.work is not None:
            self.advance(self.pending)
        return self.result


class Grid:
    def __init__(self):
        self.dp = lax.axis_size("dp")
        self.nt = lax.axis_size("tensor")
        self.nc = 2
        self.na = 4
        self.nb = self.dp // (self.na * self.nc)
        index = lax.axis_index("dp")
        self.index = index
        self.c = index % self.nc
        self.b = (index // self.nc) % self.nb
        self.a = index // (self.nc * self.nb)
        self.t = lax.axis_index("tensor")
        self.step_t = (1, self.nt)
        self.step_c = (self.nt, self.nc)
        self.step_b = (self.nt * self.nc, self.nb)
        self.step_a = (self.nt * self.nc * self.nb, self.na)

    def shift(self, value, step, amount):
        stride, size = step
        pairs = []
        for source in range(self.dp * self.nt):
            digit = (source // stride) % size
            pairs.append((source, source + ((digit + amount) % size - digit) * stride))
        return lax.ppermute(value, AXES, pairs)

    def around(self, value, step):
        held = [value]
        for _ in range(step[1] - 1):
            held.append(self.shift(held[-1], step, 1))
        return held

    def sum_around(self, part, step):
        size = step[1]
        held = part(size - 1)
        for k in range(size - 2, -1, -1):
            held = total_of(part(k), self.shift(low(held), step, -1))
        return held

    def rounds(self, value, beside=None):
        beside = beside or Beside()
        for k in range(self.na):
            ahead = self.shift(value, self.step_a, 1) if k < self.na - 1 else value
            near = self.around(value, self.step_b)
            ahead, near = beside.together((ahead, near))
            yield near
            value = ahead

    def nearby(self):
        return [
            [
                (((self.a - k) % self.na) * self.nb + (self.b - kb) % self.nb) * self.nc
                + (self.c - kc) % self.nc
                for kc in range(self.nc)
                for kb in range(self.nb)
            ]
            for k in range(self.na)
        ]

    def with_core(self, near):
        half = jnp.concatenate(near, 0)
        return jnp.concatenate([half, self.shift(half, self.step_c, 1)], 0)

    def core_sum(self, value):
        half = value.shape[0] // 2
        return low(total_of(value[:half], self.shift(value[half:], self.step_c, 1)))

    def collect_rounds(self, parts, beside=None):
        beside = beside or Beside()
        total = None
        for k in range(self.na - 1, -1, -1):
            part = parts[k]
            count = part.shape[0] // self.nb
            moved = None
            if total is not None:
                part, total = together((part, low(total)))
                moved = self.shift(total, self.step_a, -1)
            near = self.sum_around(lambda kb: part[kb * count : (kb + 1) * count], self.step_b)
            near, moved = beside.together((near, moved))
            total = near if moved is None else total_of(near, moved)
        return total

    def core_product(self, left, right):
        half = left.shape[1] // 2
        got = self.shift(low(times_over(left[:, half:], right)), self.step_c, 1)
        return low(total_of(times_over(left[:, :half], right), got))

    def scatter_ordered(self, value, beside=None):
        count = value.shape[0] // self.na
        return self.collect_rounds(
            [value[k * count : (k + 1) * count] for k in range(self.na)], beside
        )

    def long(self, value):
        return self.dp * value.shape[0] > MOST_ROWS

    def turn(self, step, value, rest, ready=None, reduce=None):
        if self.long(value):

            def advance(carry, item):
                held, total = carry
                every, item = item
                if every is None:
                    every = self.with_core(self.around(held, self.step_b))
                    held = self.shift(held, self.step_a, 1)
                part, *others = step(every, item)
                if reduce is not None:
                    total = [old + new for old, new in zip(total, reduce(item, others))]
                    others = []
                return (held, total), (part, others)

            total = []
            if reduce is not None:
                item = tuple(leaf[0] for leaf in rest)
                every = jax.ShapeDtypeStruct((rest[0].shape[1], value.shape[1]), value.dtype)
                shapes = jax.eval_shape(lambda *args: reduce(args[1], step(*args)[1:]), every, item)
                total = [jnp.zeros(shape.shape, jnp.float32) for shape in shapes]
            ready = None if ready is None else jnp.stack(ready)
            (_, total), (parts, others) = lax.scan(advance, (value, total), (ready, rest))
            return parts, (others if reduce is None else total)
        items = [tuple(leaf[k] for leaf in rest) for k in range(self.na)]
        if ready is not None:
            results = [step(*pair) for pair in zip(ready, items)]
        else:
            results = []
            for k in range(self.na):
                ahead = self.shift(value, self.step_a, 1) if k < self.na - 1 else value
                near = self.around(value, self.step_b)
                ahead, near = together((ahead, near))
                results.append(step(self.with_core(near), items[k]))
                value = ahead
        parts, *others = [list(leaves) for leaves in zip(*results)]
        return parts, others

    def gather_weight(self, value, beside=None):
        held = []
        for near in self.rounds(value, beside):
            held.extend(near)
        return self.with_core(held)

    def order(self, rows):
        at = jnp.arange(self.dp * rows, dtype=jnp.int32)
        kc, ka, kb = (
            at // (rows * self.nb * self.na),
            (at // (rows * self.nb)) % self.na,
            (at // rows) % self.nb,
        )
        a, b, c = (self.a - ka) % self.na, (self.b - kb) % self.nb, (self.c - kc) % self.nc
        source = ((a * self.nb + b) * self.nc + c) * rows + at % rows
        return low(jnp.arange(self.dp * rows, dtype=jnp.int32)[:, None] == source[None, :])

    def all_sum(self, value):
        half = value.shape[0] // 2
        keep = lax.dynamic_slice_in_dim(value, self.c * half, half, 0)
        send = lax.dynamic_slice_in_dim(value, (1 - self.c) * half, half, 0)
        yield ()
        value = keep + self.shift(send, self.step_c, 1)
        value = yield sum(self.around(value, self.step_t))
        value = yield sum(self.around(value, self.step_b))
        value = yield value + sum(self.shift(value, self.step_a, k) for k in range(1, self.na))
        other = self.shift(value, self.step_c, 1)
        return jnp.where(
            self.c == 0,
            jnp.concatenate([value, other], 0),
            jnp.concatenate([other, value], 0),
        )

    def swap(self, value):
        return self.shift(value, self.step_t, 1)

    def swap_in_turn(self, values):
        found = []
        for value in values:
            found.append(self.swap(after(value, found[-1]) if found else value))
        return found

    def pair_rows(self, value):
        other = self.swap(value)
        return jnp.where(
            self.t == 0,
            jnp.concatenate([value, other], 0),
            jnp.concatenate([other, value], 0),
        )

    def pair_sum(self, value, axis):
        half = value.shape[axis] // 2
        keep = lax.dynamic_slice_in_dim(value, self.t * half, half, axis)
        send = lax.dynamic_slice_in_dim(value, (1 - self.t) * half, half, axis)
        return total_of(keep, self.swap(low(send)))


def dense_gates(logits, picked):
    shown = jnp.where(picked, logits, -1e30)
    raised = jnp.where(picked, jnp.exp(logits - jnp.max(shown, 1, keepdims=True)), 0.0)
    return raised / jnp.sum(raised, 1, keepdims=True)


def body(
    hidden_in,
    out_grad,
    routes_first,
    routes_second,
    in_gate,
    in_value,
    in_state,
    in_step,
    mix_output,
    attn_query,
    attention_key_matrix,
    attention_value_matrix,
    attn_output,
    shared_gate_one,
    shared_up_one,
    shared_down_one,
    shared_gate_two,
    shared_up_two,
    shared_down_two,
    expert_gate_one,
    expert_up_one,
    expert_down_one,
    expert_gate_two,
    expert_up_two,
    expert_down_two,
    router_one,
    router_two,
    norm_mix,
    norm_moe_one,
    norm_attn,
    norm_moe_two,
    gated_norm,
    conv_value_weight,
    conv_value_bias,
    conv_state_weight,
    conv_state_bias,
    step_bias,
    decay_log,
    skip_gain,
):
    grid = Grid()
    tensor_rank = grid.t
    expert_count = grid.dp
    local_rows = hidden_in.shape[0]
    value_cols = in_value.shape[1]
    state_cols = in_state.shape[1]
    head_cols = in_step.shape[1]
    value_start = tensor_rank * value_cols
    state_start = tensor_rank * state_cols
    head_start = tensor_rank * head_cols
    norm_local = lax.dynamic_slice_in_dim(gated_norm, value_start, value_cols, 0)
    value_kernel = lax.dynamic_slice_in_dim(conv_value_weight, value_start, value_cols, 1)
    value_offset = lax.dynamic_slice_in_dim(conv_value_bias, value_start, value_cols, 0)
    state_kernel = lax.dynamic_slice_in_dim(conv_state_weight, state_start, state_cols, 1)
    state_offset = lax.dynamic_slice_in_dim(conv_state_bias, state_start, state_cols, 0)
    bias_local = lax.dynamic_slice_in_dim(step_bias, head_start, head_cols, 0)
    decay_local = lax.dynamic_slice_in_dim(decay_log, head_start, head_cols, 0)
    skip_local = lax.dynamic_slice_in_dim(skip_gain, head_start, head_cols, 0)
    scale = HEAD_SIZE ** (-0.5)
    model = hidden_in.shape[1]
    narrow = state_cols + head_cols
    block_rows = in_value.shape[0]

    rows = hidden_in.astype(jnp.float32)
    normalized_input, norm_pull = jax.vjp(rms_norm, rows, norm_mix)
    full = grid.pair_rows(low(normalized_input))
    sequence_length = full.shape[0]
    order = grid.order(block_rows)

    w_first = grid.gather_weight(
        jnp.concatenate(
            [in_value, in_state, in_step, jnp.zeros((block_rows, -narrow % 128), jnp.bfloat16)], 1
        )
    )
    value_weight = w_first[:, :value_cols]
    w_narrow = w_first[:, value_cols:]
    w_out_t = lax.all_gather(mix_output.T, "dp", axis=0, tiled=True)
    w_attention = lax.all_gather(
        after(
            jnp.concatenate(
                [attn_query, attention_key_matrix, attention_value_matrix, attn_output.T], 1
            ),
            w_out_t,
        ),
        "dp",
        axis=0,
        tiled=True,
    )
    q_cols = attn_query.shape[1]
    k_cols = attention_key_matrix.shape[1]
    wide_cols = q_cols + 2 * k_cols

    shared_units = shared_gate_one.shape[1] // expert_count
    shared_parts = jnp.stack(
        [
            shared_gate_one,
            shared_up_one,
            shared_down_one.T,
            shared_gate_two,
            shared_up_two,
            shared_down_two.T,
        ],
        1,
    ).reshape(block_rows, 6, expert_count, shared_units)
    shared_parts = shared_parts.transpose(2, 0, 1, 3)
    shared_own = lax.all_to_all(
        after(shared_parts.reshape(expert_count, block_rows, 6 * shared_units), w_first),
        "dp",
        split_axis=0,
        concat_axis=0,
        tiled=True,
    ).reshape(model, 6 * shared_units)
    shared_other = grid.swap(shared_own)

    def shared_of(which):
        at = which * shared_units
        return [
            shared_own[:, at : at + shared_units],
            shared_other[:, at : at + shared_units],
        ]

    def expert_weights(bank, which, when):
        own = [leaf[0] for leaf in bank]
        gate_other, up_other, down_other = grid.swap_in_turn(after(own, when))
        gate_own, up_own, down_own = own
        narrow_in = together(jnp.concatenate(shared_of(which) + shared_of(which + 1), 1))
        w_in = jnp.concatenate([gate_own, gate_other, up_own, up_other, narrow_in], 1)
        down_t = jnp.concatenate(shared_of(which + 2), 1)
        w_down = jnp.concatenate([down_own, down_other, down_t.T], 0)
        return w_in, w_down

    experts_one = expert_weights((expert_gate_one, expert_up_one, expert_down_one), 0, full)
    half_units = expert_gate_one.shape[2]
    units = 2 * half_units
    pair_units = 2 * shared_units

    def local_mask(routes):
        mine = lax.dynamic_slice_in_dim(routes, tensor_rank * local_rows, local_rows, 0)
        names = jnp.arange(expert_count, dtype=jnp.int32)
        return jnp.any(mine[:, :, None] == names[None, None, :], 1)

    mask_one, mask_two = local_mask(routes_first), local_mask(routes_second)
    masks = low(jnp.concatenate([mask_one, mask_two], 1))
    spare_columns = max(0, MASK_COLUMNS - masks.shape[1])
    masks = lax.all_gather(jnp.pad(masks, ((0, 0), (0, spare_columns))), "dp", axis=0)
    masks = [
        jnp.concatenate([masks[at, :, : 2 * expert_count] for at in blocks], 0) > 0.5
        for blocks in grid.nearby()
    ]
    picked_one = jnp.stack([mask[:, :expert_count] for mask in masks])
    picked_two = jnp.stack([mask[:, expert_count:] for mask in masks])
    here = (jnp.arange(expert_count, dtype=jnp.int32) == grid.index)[None, :]

    def split_up(before):
        wide = before.astype(jnp.float32)
        edges = [units, 2 * units, 2 * units + pair_units]
        return jnp.split(wide, edges, 1)

    def moe_forward(rows, gain, router, picked, weights):
        w_in, w_down = weights
        normalized_input, norm_pull = jax.vjp(rms_norm, rows, gain)
        local = low(normalized_input)

        def step(every, chunk):
            (chosen,) = chunk
            gates = dense_gates(matmul(every, router), chosen)
            gate = jnp.sum(jnp.where(here, gates, 0.0), 1, keepdims=True)
            before = low(matmul(every, w_in))
            first, second, shared_a, shared_b = split_up(before)
            hidden = jnp.concatenate(
                [
                    low(jax.nn.silu(first) * second * gate),
                    low(jax.nn.silu(shared_a) * shared_b),
                ],
                1,
            )
            part = grid.core_sum(low(matmul(hidden, w_down)))
            return (part, every, gate, before, hidden)

        parts, kept = grid.turn(step, local, (picked,))
        return parts, (norm_pull, local, kept)

    def moe_backward(grad, router, local_picked, weights, keep, ready=None):
        w_in, w_down = weights
        norm_pull, local, kept = keep
        spare = jnp.arange(SPARE, dtype=jnp.int32)[None, :] == grid.index

        def step(d_every, chunk):
            _, gate, before, _ = chunk
            first, second, shared_a, shared_b = split_up(before)
            d_before = low(times_back(d_every, w_down)).astype(jnp.float32)
            d_hidden, d_shared = d_before[:, :units], d_before[:, units:]
            active = jax.nn.silu(first)
            d_gate = jnp.sum(d_hidden * active * second, 1, keepdims=True)
            d_hidden = d_hidden * gate
            d_in = jnp.concatenate(
                [
                    low(d_hidden * second * silu_slope(first)),
                    low(d_hidden * active),
                    low(d_shared * shared_b * silu_slope(shared_a)),
                    low(d_shared * jax.nn.silu(shared_a)),
                ],
                1,
            )
            d_in = together(d_in)
            sent = jnp.concatenate(
                [low(times_back(d_in, w_in)), low(jnp.where(spare, d_gate, 0.0))], 1
            )
            return (grid.core_sum(sent), d_every, d_in)

        def reduce(chunk, more):
            every, _, _, hidden = chunk
            d_every, d_in = more
            return times_over(every, d_in), times_over(hidden, d_every)

        parts, others = grid.turn(step, low(grad), kept, ready, reduce)
        if grid.long(grad):
            got = grid.collect_rounds(parts)
            g_in, g_down = others
        else:
            got = grid.collect_rounds(parts)
        others = others if grid.long(grad) else (kept[0], kept[3], *others)
        gates = dense_gates(matmul(local, router), local_picked)
        d_gates = got[:, model : model + expert_count]
        d_logits = low(gates * (d_gates - jnp.sum(gates * d_gates, 1, keepdims=True)))
        d_local = got[:, :model] + times_back(d_logits, router)
        g_router = times_over(d_logits, local)
        d_rows, g_gain = norm_pull(d_local)
        return (grad + d_rows, g_gain, g_router, others)

    def expert_grads(others, when):
        if len(others) == 2:
            g_in, g_down = others
        else:
            every, hidden, d_every, d_in = [
                jnp.concatenate(list(leaf), 0) for leaf in after(others, when)
            ]
            g_in, g_down = times_over(every, d_in), times_over(hidden, d_every)
        own, other = slice(0, half_units), slice(half_units, units)
        own_up = slice(units, units + half_units)
        other_up = slice(units + half_units, 2 * units)
        g_rest, g_rest_down = g_in[:, 2 * units :], g_down[units:].T
        s = shared_units
        mine = jnp.concatenate([g_rest[:, :s], g_rest[:, 2 * s : 3 * s], g_rest_down[:, :s]], 1)
        theirs = jnp.concatenate([g_rest[:, s : 2 * s], g_rest[:, 3 * s :], g_rest_down[:, s:]], 1)
        theirs, g_gate_other, g_up_other, g_down_other = grid.swap_in_turn(
            (low(theirs), low(g_in[:, other]), low(g_in[:, other_up]), low(g_down[other]))
        )
        g_shared = low(mine + theirs)
        g_experts = (
            (g_in[:, own] + g_gate_other)[None],
            (g_in[:, own_up] + g_up_other)[None],
            (g_down[own] + g_down_other)[None],
        )
        return g_shared, g_experts

    def sum_weight(value):
        return lax.psum_scatter(value, "dp", scatter_dimension=0, tiled=True).astype(jnp.float32)

    heads = head_cols
    block_count = sequence_length // CH

    def cut(value):
        return [value[at * CH : (at + 1) * CH] for at in range(block_count)]

    def mixer_forward():
        ordered = low(matmul(full, order))
        value_pre = matmul(ordered, value_weight)
        narrow_pre = matmul(ordered, w_narrow)
        state_pre = narrow_pre[:, :state_cols]
        step_pre = narrow_pre[:, state_cols:narrow]
        value_act, value_pull = jax.vjp(conv_act, value_pre, value_kernel, value_offset)
        state_act, state_pull = jax.vjp(conv_act, state_pre, state_kernel, state_offset)
        state_own = low(state_act)
        state_other = grid.swap(state_own)
        value_act, state_own, state_other = yield (value_act, state_own, state_other)
        in_map = jnp.where(tensor_rank == 0, state_own, state_other).astype(jnp.float32)
        out_map = jnp.where(tensor_rank == 0, state_other, state_own).astype(jnp.float32)
        state, outs, pulls = None, [], []
        cuts = zip(cut(value_act.reshape(sequence_length, heads, -1)), cut(step_pre), cut(in_map), cut(out_map))
        for at, (x_blk, step_blk, b_blk, c_blk) in enumerate(cuts):
            more = at < block_count - 1

            def block(x_blk, step_blk, bias, decay, skip, b_blk, c_blk, state, more=more):
                return scan_block(x_blk, step_blk, bias, decay, skip, b_blk, c_blk, state, more)

            (state, out), pull = jax.vjp(
                block, x_blk, step_blk, bias_local, decay_local, skip_local, b_blk, c_blk, state
            )
            state, out = yield (state, out)
            outs.append(out.reshape(CH, -1))
            pulls.append(pull)
        return ordered, jnp.concatenate(outs, 0), value_pull, state_pull, pulls

    work = Beside(mixer_forward())
    w_gate = grid.gather_weight(after(in_gate, w_first), work)
    ordered, ssm_out, value_pull, state_pull, scan_pulls = work.finish()

    gate_pre = matmul(ordered, w_gate)
    gated = ssm_out * jax.nn.silu(gate_pre)
    square = jnp.sum(gated * gated, 1, keepdims=True)
    inverse = lax.rsqrt((square + grid.swap(square)) / DI + EPS)
    mixed = low(gated * inverse * norm_local)
    mixed_out = times_back(mixed, w_out_t)
    result = rows + grid.pair_sum(mixed_out, 0)
    experts_two = expert_weights((expert_gate_two, expert_up_two, expert_down_two), 3, result)
    qkv_weight = w_attention[:, :wide_cols]
    attn_out_t = w_attention[:, wide_cols:]
    parts, moe_one_keep = moe_forward(result, norm_moe_one, router_one, picked_one, experts_one)
    parts, experts_two = together((parts, experts_two))
    state_two = result + grid.collect_rounds(parts)

    normalized_input, attention_norm_pull = jax.vjp(rms_norm, state_two, norm_attn)
    attention_full = grid.pair_rows(low(normalized_input))
    kv_heads = k_cols // HEAD_SIZE
    query_groups = QUERY_HEADS // KEY_VALUE_HEADS

    def attention_forward():
        qkv = low(matmul(attention_full, qkv_weight))
        query_rows = qkv[:, :q_cols].reshape(sequence_length, kv_heads, query_groups, HEAD_SIZE)
        key_rows = qkv[:, q_cols : q_cols + k_cols].reshape(sequence_length, kv_heads, HEAD_SIZE)
        value_rows = qkv[:, q_cols + k_cols :].reshape(sequence_length, kv_heads, HEAD_SIZE)
        causal = jnp.arange(sequence_length)[:, None] >= jnp.arange(sequence_length)[None, :]
        scores = (
            jnp.einsum("ikgd,jkd->kgij", query_rows, key_rows, preferred_element_type=jnp.float32)
            * scale
        )
        scores = jnp.where(causal, scores, -1e30)
        peak = jnp.max(scores, 3, keepdims=True)
        raised = jnp.exp(scores - peak)
        probs = yield raised / jnp.sum(raised, 3, keepdims=True)
        low_probs = low(probs)
        attended = jnp.einsum(
            "kgij,jkd->ikgd", low_probs, value_rows, preferred_element_type=jnp.float32
        )
        attended = low(attended.reshape(sequence_length, -1))
        output = yield grid.pair_sum(times_back(attended, attn_out_t), 0)
        return query_rows, key_rows, value_rows, probs, low_probs, attended, state_two + output

    work = Beside(attention_forward())
    d_every_two = [
        grid.with_core(near) for near in grid.rounds(after(out_grad, attention_full), work)
    ]
    query_rows, key_rows, value_rows, probs, low_probs, attended, result = work.finish()
    output_parts, moe_two_keep = moe_forward(
        result, norm_moe_two, router_two, picked_two, experts_two
    )
    forward_rows = result

    grad = out_grad.astype(jnp.float32)
    grad, g_nmoe_two, g_router_two, weights_two = moe_backward(
        grad, router_two, mask_two, experts_two, moe_two_keep, d_every_two
    )
    g_shared_two, g_experts_two = expert_grads(weights_two, grad)

    dfull = grid.pair_rows(low(grad))

    def attention_backward():
        d_att = low(matmul(dfull, attn_out_t)).reshape(query_rows.shape)
        d_probs = jnp.einsum(
            "ikgd,jkd->kgij", d_att, value_rows, preferred_element_type=jnp.float32
        )
        d_scores = low(probs * (d_probs - jnp.sum(probs * d_probs, 3, keepdims=True)))
        d_att, d_scores = yield (d_att, d_scores)
        d_query = low(
            jnp.einsum("kgij,jkd->ikgd", d_scores, key_rows, preferred_element_type=jnp.float32)
            * scale
        ).reshape(sequence_length, -1)
        d_keys = low(
            jnp.einsum("kgij,ikgd->jkd", d_scores, query_rows, preferred_element_type=jnp.float32)
            * scale
        ).reshape(sequence_length, -1)
        d_values = low(
            jnp.einsum("kgij,ikgd->jkd", low_probs, d_att, preferred_element_type=jnp.float32)
        ).reshape(sequence_length, -1)
        d_qkv = jnp.concatenate([d_query, d_keys, d_values], 1)
        d_qkv, d_normed = yield (d_qkv, grid.pair_sum(times_back(d_qkv, qkv_weight), 0))
        g_out_t = low(times_over(dfull, attended))
        g_qkv = low(times_over(attention_full, d_qkv))
        g_all = yield jnp.concatenate([g_qkv, g_out_t], 1)
        return d_normed, g_all

    work = Beside(attention_backward())
    output_parts, dfull = together((output_parts, dfull))
    block_out = forward_rows + grid.collect_rounds(output_parts, work)
    d_normed, g_attention = work.finish()
    attention_sum = sum_weight(g_attention)
    d_rows, g_nattn = attention_norm_pull(d_normed)
    grad = grad + d_rows

    grad, g_nmoe_one, g_router_one, weights_one = moe_backward(
        grad, router_one, mask_one, experts_one, moe_one_keep
    )

    dfull, g_experts_two = together((grid.pair_rows(low(grad)), g_experts_two))
    kept_gate = []

    def mixer_backward():
        d_mixed = matmul(dfull, w_out_t)
        weighted = d_mixed * norm_local
        total = jnp.sum(weighted * gated, 1, keepdims=True)
        total = total + grid.swap(total)
        d_gated = weighted * inverse - gated * inverse**3 * (total / DI)
        g_ngated = jnp.sum(d_mixed * gated * inverse, 0)
        d_ssm, low_gate = yield (
            d_gated * jax.nn.silu(gate_pre),
            low(d_gated * ssm_out * silu_slope(gate_pre)),
        )
        kept_gate.append(low_gate)
        d_state, back = None, []
        for pull, d_out in list(zip(scan_pulls, cut(d_ssm.reshape(sequence_length, heads, -1))))[::-1]:
            *found, d_state = yield pull((d_state, d_out))
            back.append(found)
        d_x, d_step, g_bias, g_decay, g_skip, d_in_map, d_out_map = zip(*back[::-1])
        d_value_act = jnp.concatenate(d_x, 0).reshape(sequence_length, -1)
        d_step = jnp.concatenate(d_step, 0)
        d_in_map, d_out_map = jnp.concatenate(d_in_map, 0), jnp.concatenate(d_out_map, 0)
        g_bias, g_decay, g_skip = sum(g_bias), sum(g_decay), sum(g_skip)
        map_keep = jnp.where(tensor_rank == 0, d_in_map, d_out_map)
        map_send = jnp.where(tensor_rank == 0, d_out_map, d_in_map)
        d_state_act = total_of(map_keep, grid.swap(low(map_send)))
        d_value, g_vkernel, g_voffset = value_pull(d_value_act)
        d_value, d_state_act = yield (low(d_value), d_state_act)
        d_state, g_skernel, g_soffset = state_pull(d_state_act)
        low_narrow = jnp.concatenate(
            [low(d_state), low(d_step), jnp.zeros((sequence_length, -narrow % 128), jnp.bfloat16)],
            1,
        )
        smalls = (g_ngated, g_vkernel, g_voffset, g_skernel, g_soffset, g_bias, g_decay, g_skip)
        return jnp.concatenate([d_value, low_narrow], 1), smalls

    mix_out_sum = sum_weight(after(low(times_over(dfull, mixed)), attention_sum))
    low_first, smalls = Beside(mixer_backward()).finish()
    (low_gate,) = kept_gate
    gate_sum = sum_weight(after(low(times_over(full, low_gate)), mix_out_sum))
    late_sums = grid.core_product(ordered, low_first)
    low_gate, low_first = after((low_gate, low_first), late_sums)
    d_normed = times_back(low_gate, w_gate) + times_back(low_first, w_first)
    d_normed = times_back(low(d_normed), order)
    d_rows, g_nmix = norm_pull(grid.pair_sum(d_normed, 0))
    grad = grad + d_rows
    g_ngated, g_vkernel, g_voffset, g_skernel, g_soffset, g_bias, g_decay, g_skip = smalls

    g_shared_one, g_experts_one = expert_grads(weights_one, low_first)
    shared_grads = jnp.concatenate([g_shared_one, g_shared_two], 1)
    shared_back = lax.all_to_all(
        shared_grads.reshape(expert_count, block_rows, 6 * shared_units),
        "dp",
        split_axis=0,
        concat_axis=0,
        tiled=True,
    ).astype(jnp.float32)
    shared_back = shared_back.reshape(expert_count, block_rows, 6, shared_units)
    shared_back = shared_back.transpose(2, 1, 0, 3).reshape(6, block_rows, -1)

    def spread(value, start, whole):
        value = value.reshape(-1, value.shape[-1])
        wide = jnp.zeros((value.shape[0], whole), jnp.float32)
        return lax.dynamic_update_slice_in_dim(wide, value, start, 1).reshape(-1)

    def pack_sums(pieces):
        packed = [piece.reshape(-1) for piece in pieces]
        packed.append(jnp.zeros((-sum(piece.size for piece in pieces) % 2048,), jnp.float32))
        return Beside(grid.all_sum(jnp.concatenate(packed).reshape(-1, 128)))

    def unpack_sums(work, pieces):
        packed, found, at = work.finish().reshape(-1), [], 0
        for piece in pieces:
            found.append(packed[at : at + piece.size])
            at += piece.size
        return found

    early = (g_router_one, g_router_two, g_nmoe_one, g_nattn, g_nmoe_two)
    late = (
        g_nmix,
        spread(g_ngated, value_start, DI),
        spread(g_vkernel, value_start, DI),
        spread(g_voffset, value_start, DI),
        spread(g_skernel, state_start, 2 * NS),
        spread(g_soffset, state_start, 2 * NS),
        spread(g_bias, head_start, MH),
        spread(g_decay, head_start, MH),
        spread(g_skip, head_start, MH),
    )
    early = unpack_sums(pack_sums(early), early)
    work = pack_sums(late)
    value_sum = grid.scatter_ordered(late_sums, work)
    late = unpack_sums(work, late)
    summed = early[:2] + late[:1] + early[2:] + late[1:]
    return (
        block_out,
        grad,
        gate_sum,
        value_sum[:, :value_cols],
        value_sum[:, value_cols : value_cols + state_cols],
        value_sum[:, value_cols + state_cols : value_cols + narrow],
        mix_out_sum.T,
        attention_sum[:, :q_cols],
        attention_sum[:, q_cols : q_cols + k_cols],
        attention_sum[:, q_cols + k_cols : wide_cols],
        attention_sum[:, wide_cols:].T,
        shared_back[0],
        shared_back[1],
        shared_back[2].T,
        shared_back[3],
        shared_back[4],
        shared_back[5].T,
        g_experts_one[0],
        g_experts_one[1],
        g_experts_one[2],
        g_experts_two[0],
        g_experts_two[1],
        g_experts_two[2],
        summed[0].reshape(expert_count, model).T,
        summed[1].reshape(expert_count, model).T,
        summed[2],
        summed[3],
        summed[4],
        summed[5],
        summed[6],
        summed[7].reshape(-1, DI),
        summed[8],
        summed[9].reshape(-1, 2 * NS),
        summed[10],
        summed[11],
        summed[12],
        summed[13],
    )


def solution(mesh):
    in_specs = (
        P(("dp", "tensor"), None),
        P(("dp", "tensor"), None),
        P("dp", None),
        P("dp", None),
        P("dp", "tensor"),
        P("dp", "tensor"),
        P("dp", "tensor"),
        P("dp", "tensor"),
        P("tensor", "dp"),
        P("dp", "tensor"),
        P("dp", "tensor"),
        P("dp", "tensor"),
        P("tensor", "dp"),
        P("dp", "tensor"),
        P("dp", "tensor"),
        P("tensor", "dp"),
        P("dp", "tensor"),
        P("dp", "tensor"),
        P("tensor", "dp"),
        P("dp", None, "tensor"),
        P("dp", None, "tensor"),
        P("dp", "tensor", None),
        P("dp", None, "tensor"),
        P("dp", None, "tensor"),
        P("dp", "tensor", None),
        P(),
        P(),
        P(),
        P(),
        P(),
        P(),
        P(),
        P(),
        P(),
        P(),
        P(),
        P(),
        P(),
        P(),
    )
    out_specs = (
        P(("dp", "tensor"), None),
        P(("dp", "tensor"), None),
        P("dp", "tensor"),
        P("dp", "tensor"),
        P("dp", "tensor"),
        P("dp", "tensor"),
        P("tensor", "dp"),
        P("dp", "tensor"),
        P("dp", "tensor"),
        P("dp", "tensor"),
        P("tensor", "dp"),
        P("dp", "tensor"),
        P("dp", "tensor"),
        P("tensor", "dp"),
        P("dp", "tensor"),
        P("dp", "tensor"),
        P("tensor", "dp"),
        P("dp", None, "tensor"),
        P("dp", None, "tensor"),
        P("dp", "tensor", None),
        P("dp", None, "tensor"),
        P("dp", None, "tensor"),
        P("dp", "tensor", None),
        P(),
        P(),
        P(),
        P(),
        P(),
        P(),
        P(),
        P(),
        P(),
        P(),
        P(),
        P(),
        P(),
        P(),
    )
    return jax.shard_map(body, mesh=mesh, in_specs=in_specs, out_specs=out_specs, check_vma=False)
```
